32 devices in a mesh: group: 2 (over core), member: 16 (over z, y, x).
Axes of the slice: x: 2, y: 2, z: 4, core: 2. Of those that a mesh axis runs over, the one named last changes fastest.
Arguments:
- features: bfloat16 [65536, 256], P(('group', 'member')), may hold values from -6 to 6
- local_home: int32 [2048], P(('group', 'member')), may hold values from 0 to 15
- local_near: int32 [2048], P(('group', 'member')), may hold values from 0 to 15
- local_tiles: bfloat16 [2048, 128, 128], P(('group', 'member')), may hold values from -0.125 to 0.125
- remote_home: int32 [512], P(('group', 'member')), may hold values from 0 to 15
- remote_far: int32 [512], P(('group', 'member')), may hold values from 0 to 511, as said below
- remote_tiles: bfloat16 [512, 128, 128], P(('group', 'member')), may hold values from -0.125 to 0.125
- weight: bfloat16 [512, 256], replicated, may hold values from -0.25 to 0.25
- cotangent: bfloat16 [65536, 256], P(('group', 'member')), may hold values from -6 to 6
Outputs:
- output: bfloat16 [65536, 256], P(('group', 'member'))
- grad_weight: float32 [512, 256], replicated
- grad_features: float32 [65536, 256], P(('group', 'member'))
The draws below stay inside these ranges and needn't reach their ends.
Inputs may be any that keep to these rules, and one draw needn't show every extreme that they name: `remote_far`: the remote pairs of one owner name partner blocks on 16 different owners other than itself, one block from each owner; one owner, drawn from the seed, holds a partner block of every other owner's remote pairs.
All inputs are finite; a program needn't handle non-finite values.
Results may differ from the reference program's by a relative error of at most 0.0057.
Values may be sent and summed in bfloat16 or wider, within the bound.
A program may use at most 192 MiB of HBM per device.

```python
import jax
import jax.numpy as jnp
from jax import lax

F = 256
BLOCK = 128
BLK_DEV = 16
LOCAL_DEV = 64
REMOTE_DEV = 16
ITEMS = 65536
DEVICES = 32


def draw_remote_far(key, part):
    target = jax.random.randint(jax.random.fold_in(key, 7), (), 0, DEVICES)
    device_keys = jax.random.split(jax.random.fold_in(key, 11), DEVICES)
    owners = jnp.arange(DEVICES, dtype=jnp.int32)

    def one_device(dev_key, self_index):
        positions = jnp.arange(DEVICES, dtype=jnp.int32)
        scores = jax.random.permutation(dev_key, DEVICES).astype(jnp.int32)
        scores = jnp.where(positions == target, -1, scores)
        scores = jnp.where(positions == self_index, DEVICES + 5, scores)
        chosen = jnp.argsort(scores, stable=True)[:REMOTE_DEV].astype(jnp.int32)
        offset = jax.random.randint(jax.random.fold_in(dev_key, 3), (REMOTE_DEV,), 0, BLK_DEV)
        return (chosen * BLK_DEV + offset).astype(jnp.int32)
    return jax.vmap(one_device)(device_keys, owners).reshape(-1)


def place_ends(entries, rng, low, top_value):
    index_at = [jax.random.randint(jax.random.fold_in(rng, axis), (), 0, length) for axis, length in enumerate(entries.shape)]
    widest = entries.shape.index(max(entries.shape))
    neighbour = index_at[:widest] + [(index_at[widest] + 1) % entries.shape[widest]] + index_at[widest + 1:]
    return entries.at[tuple(index_at)].set(low).at[tuple(neighbour)].set(top_value)


def block_levels(key, extent, cuts, least, high):
    loudness = 1.0
    for axis_at, blocks in cuts:
        heights = jax.random.uniform(jax.random.fold_in(jax.random.fold_in(key, 6), axis_at), (blocks,), jnp.float32, least / len(cuts), high / len(cuts))
        loudness = loudness * jnp.repeat(jnp.exp(heights), extent[axis_at] // blocks).reshape((-1,) + (1,) * (len(extent) - 1 - axis_at))
    return loudness


def bell_draw(rng, shape, width, limit, shards=(), kind=jnp.bfloat16):
    gain = block_levels(rng, shape, shards, -0.22, 0.18) if shards else 1.0
    drawn = jax.random.normal(rng, shape, jnp.float32) * width * gain
    return jnp.minimum(jnp.maximum(drawn, -limit), limit).astype(kind)


def setup_inputs(seed: int = 0) -> dict:
    splits = jax.random.split(jax.random.key(seed), 10)
    features = bell_draw(splits[0], (ITEMS, F), 1.0, 6.0, ((0, 32),))
    local_home = place_ends(jax.random.randint(splits[1], (DEVICES * LOCAL_DEV,), 0, BLK_DEV), jax.random.fold_in(splits[1], 1), 0, BLK_DEV - 1).astype(jnp.int32)
    local_near = place_ends(jax.random.randint(splits[2], (DEVICES * LOCAL_DEV,), 0, BLK_DEV), jax.random.fold_in(splits[2], 1), 0, BLK_DEV - 1).astype(jnp.int32)
    local_tiles = bell_draw(splits[3], (DEVICES * LOCAL_DEV, BLOCK, BLOCK), (BLOCK * 16) ** -0.5, 0.125, ((0, 32),))
    remote_home = place_ends(jax.random.randint(splits[4], (DEVICES * REMOTE_DEV,), 0, BLK_DEV), jax.random.fold_in(splits[4], 1), 0, BLK_DEV - 1).astype(jnp.int32)
    remote_far = draw_remote_far(jax.random.fold_in(splits[9], 71), 0)
    remote_tiles = bell_draw(splits[6], (DEVICES * REMOTE_DEV, BLOCK, BLOCK), (BLOCK * 16) ** -0.5, 0.125, ((0, 32),))
    weight = bell_draw(splits[7], (2 * F, F), (2 * F) ** -0.5, 0.25)
    cotangent = bell_draw(splits[8], (ITEMS, F), 1.0, 6.0, ((0, 32),))
    return {"features": features, "local_home": local_home, "local_near": local_near, "local_tiles": local_tiles, "remote_home": remote_home, "remote_far": remote_far, "remote_tiles": remote_tiles, "weight": weight, "cotangent": cotangent}


def spread(index_list, count):
    return (index_list[:, None] == jnp.arange(count, dtype=jnp.int32)[None, :]).astype(jnp.float32)

def apply_graph(field, local_home, local_near, local_tiles, remote_home, remote_far, remote_tiles):
    field_dev = field.reshape(DEVICES, BLK_DEV, BLOCK, F)
    whole = field.reshape(DEVICES * BLK_DEV, BLOCK, F)
    inputs = (field_dev, local_home.reshape(DEVICES, LOCAL_DEV), local_near.reshape(DEVICES, LOCAL_DEV), local_tiles.reshape(DEVICES, LOCAL_DEV, BLOCK, BLOCK), remote_home.reshape(DEVICES, REMOTE_DEV), remote_far.reshape(DEVICES, REMOTE_DEV), remote_tiles.reshape(DEVICES, REMOTE_DEV, BLOCK, BLOCK))

    def one_owner(far_total, item):
        own, home_l, near_l, tiles_l, home_r, far_r, tiles_r = item
        own_f = own.astype(jnp.float32)
        tl = tiles_l.astype(jnp.float32)
        tr = tiles_r.astype(jnp.float32)
        to_home = jnp.einsum('pab,pbf->paf', tl, own_f[near_l], precision=lax.Precision.HIGHEST)
        to_near = jnp.einsum('pba,pbf->paf', tl, own_f[home_l], precision=lax.Precision.HIGHEST)
        far_vals = whole[far_r].astype(jnp.float32)
        to_home_r = jnp.einsum('pab,pbf->paf', tr, far_vals, precision=lax.Precision.HIGHEST)
        to_far = jnp.einsum('pba,pbf->paf', tr, own_f[home_r], precision=lax.Precision.HIGHEST)
        to_far = to_far.astype(jnp.bfloat16).astype(jnp.float32)
        local_sum = jnp.einsum('pk,paf->kaf', spread(home_l, BLK_DEV), to_home, precision=lax.Precision.HIGHEST)
        local_sum = local_sum + jnp.einsum('pk,paf->kaf', spread(near_l, BLK_DEV), to_near, precision=lax.Precision.HIGHEST)
        local_sum = local_sum + jnp.einsum('pk,paf->kaf', spread(home_r, BLK_DEV), to_home_r, precision=lax.Precision.HIGHEST)
        far_total = far_total.at[far_r].add(to_far)
        return (far_total, local_sum)
    start = jnp.zeros((DEVICES * BLK_DEV, BLOCK, F), jnp.float32)
    far_total, local_sums = lax.scan(one_owner, start, inputs)
    result = local_sums.reshape(DEVICES * BLK_DEV, BLOCK, F) + far_total
    return result.reshape(ITEMS, F)

def reference(features, local_home, local_near, local_tiles, remote_home, remote_far, remote_tiles, weight, cotangent):
    graph_args = (local_home, local_near, local_tiles, remote_home, remote_far, remote_tiles)
    aggregate = apply_graph(features, *graph_args).astype(jnp.bfloat16)
    joined = jnp.concatenate([features, aggregate], axis=1)
    pre_act = jnp.dot(joined, weight, preferred_element_type=jnp.float32)
    sigmoid_z = jax.nn.sigmoid(pre_act)
    output = (pre_act * sigmoid_z).astype(jnp.bfloat16)
    grad_pre = (cotangent.astype(jnp.float32) * sigmoid_z * (1.0 + pre_act * (1.0 - sigmoid_z))).astype(jnp.bfloat16)
    grad_scale = 1.0 / jnp.sqrt(jnp.float32(ITEMS))
    grad_weight = jnp.dot(joined.T, grad_pre, preferred_element_type=jnp.float32) * grad_scale
    grad_joined = jnp.dot(grad_pre, weight.T, preferred_element_type=jnp.float32)
    grad_agg = grad_joined[:, F:].astype(jnp.bfloat16)
    grad_features = grad_joined[:, :F] + apply_graph(grad_agg, *graph_args)
    return (output, grad_weight, grad_features)
```

```python
import functools
import math

import jax
import jax.numpy as jnp
from jax import lax
from jax.experimental import pallas as pl
from jax.experimental.pallas import tpu as pltpu
from jax.sharding import PartitionSpec as P

BLOCK = 128
BLK_DEV = 16
AXES = ("group", "member")
VMEM = pl.BlockSpec(memory_space=pltpu.VMEM)
SMEM = pl.BlockSpec(memory_space=pltpu.SMEM)
LIMIT = 56 * 1024 * 1024


def dot(a, b):
    return jnp.dot(a, b, preferred_element_type=jnp.float32)


def dot_lt(a, b):
    return lax.dot_general(a, b, (((0,), (0,)), ((), ())), preferred_element_type=jnp.float32)


def dot_rt(a, b):
    return lax.dot_general(a, b, (((1,), (1,)), ((), ())), preferred_element_type=jnp.float32)


def fill_send(v, asked, home_r, target, tiles_r, send):
    @pl.loop(0, send.shape[0])
    def _(j):
        send[j, :BLOCK] = v[jnp.maximum(asked[j], 0)]

    @pl.loop(0, tiles_r.shape[0])
    def _(p):
        send[target[p], BLOCK:] = dot_lt(tiles_r[p], v[home_r[p]]).astype(jnp.bfloat16)


def add_remote(acc, arrived, asked, home_r, target, tiles_r):
    @pl.loop(0, tiles_r.shape[0])
    def _(p):
        acc[home_r[p]] += dot(tiles_r[p], arrived[target[p], :BLOCK])

    @pl.loop(0, arrived.shape[0])
    def _(j):
        @pl.when(asked[j] >= 0)
        def _():
            acc[asked[j]] += arrived[j, BLOCK:].astype(jnp.float32)


def send_kernel(asked, home_r, target, v, tiles_r, send):
    fill_send(v, asked, home_r, target, tiles_r, send)


def local_kernel(home, near, v, tiles, base, acc):
    acc[...] = jnp.zeros_like(acc) if base is None else base[...]

    @pl.loop(0, tiles.shape[0], unroll=2)
    def _(p):
        h, n = home[p], near[p]
        tile = tiles[p]
        acc[h] += dot(tile, v[n])
        acc[n] += dot_lt(tile, v[h])


def middle_kernel(
    asked, home_r, target, arrived, local, tiles_r, feats, weight, cot,
    out, base, grad_agg, partial, send, acc,
):
    width = feats.shape[-1]
    acc[...] = local[...]
    add_remote(acc, arrived, asked, home_r, target, tiles_r)
    partial[...] = jnp.zeros_like(partial)
    step = 4
    rows = step * BLOCK

    @pl.loop(0, feats.shape[0] // step)
    def _(i):
        sl = pl.ds(i * step, step)
        f = feats[sl].reshape(rows, width)
        a = acc[sl].reshape(rows, width).astype(jnp.bfloat16)
        z = dot(f, weight[:width]) + dot(a, weight[width:])
        s = jax.nn.sigmoid(z)
        out[sl] = (z * s).astype(jnp.bfloat16).reshape(step, BLOCK, width)
        c = cot[sl].reshape(rows, width).astype(jnp.float32)
        g = (c * s * (1.0 + z * (1.0 - s))).astype(jnp.bfloat16)
        partial[:width] += dot_lt(f, g)
        partial[width:] += dot_lt(a, g)
        base[sl] = dot_rt(g, weight[:width]).reshape(step, BLOCK, width)
        grad_agg[sl] = dot_rt(g, weight[width:]).astype(jnp.bfloat16).reshape(step, BLOCK, width)

    fill_send(grad_agg, asked, home_r, target, tiles_r, send)


def final_kernel(asked, home_r, target, arrived, local, tiles_r, out):
    out[...] = local[...]
    add_remote(out, arrived, asked, home_r, target, tiles_r)


def call(kernel, out_shape, n_smem, n_vmem, scratch=(), flops=0, moved=0):
    return pl.pallas_call(
        kernel,
        out_shape=out_shape,
        in_specs=[SMEM] * n_smem + [VMEM] * n_vmem,
        out_specs=jax.tree.map(lambda _: VMEM, out_shape),
        scratch_shapes=list(scratch),
        compiler_params=pltpu.CompilerParams(vmem_limit_bytes=LIMIT),
        cost_estimate=pl.CostEstimate(flops=flops, bytes_accessed=moved, transcendentals=0),
    )


def exchange(buffer):
    return lax.all_to_all(buffer, AXES, split_axis=0, concat_axis=0, tiled=True)


def body(
    features, local_home, local_near, local_tiles, remote_home, remote_far, remote_tiles, weight, cotangent
):
    devices = lax.axis_size(AXES)
    row_count, width = features.shape
    blocks = row_count // BLOCK
    bf16, f32 = jnp.bfloat16, jnp.float32
    shaped = lambda dtype: jax.ShapeDtypeStruct((blocks, BLOCK, width), dtype)
    send_shape = jax.ShapeDtypeStruct((devices, 2 * BLOCK, width), bf16)
    target = remote_far // BLK_DEV
    request = jnp.full((devices,), -1, jnp.int32).at[target].set(remote_far % BLK_DEV)
    asked = exchange(request)
    idx = (asked, remote_home, target)
    feats = features.reshape(blocks, BLOCK, width)
    cot = cotangent.reshape(blocks, BLOCK, width)
    local_flops = 4 * BLOCK * BLOCK * width * local_tiles.shape[0]

    send1 = call(send_kernel, send_shape, 3, 2)(*idx, feats, remote_tiles)
    arrived1 = exchange(send1)
    first_local = lambda h, n, v, t, acc: local_kernel(h, n, v, t, None, acc)
    local1 = call(first_local, shaped(f32), 2, 2, flops=20 * local_flops, moved=20 << 20)(
        local_home, local_near, feats, local_tiles
    )
    out, base, grad_agg, partial, send2 = call(
        middle_kernel,
        (shaped(bf16), shaped(f32), shaped(bf16), jax.ShapeDtypeStruct(weight.shape, f32), send_shape),
        3,
        6,
        scratch=[pltpu.VMEM((blocks, BLOCK, width), f32)],
    )(*idx, arrived1, local1, remote_tiles, feats, weight, cot)
    arrived2 = exchange(send2)
    local2 = call(local_kernel, shaped(f32), 2, 3, flops=20 * local_flops, moved=20 << 20)(
        local_home, local_near, grad_agg, local_tiles, base
    )
    grad_scale = 1.0 / math.sqrt(row_count * devices)
    grad_weight = lax.psum(partial, AXES) * grad_scale
    grad_features = call(final_kernel, shaped(f32), 3, 3)(*idx, arrived2, local2, remote_tiles)
    return (
        out.reshape(row_count, width),
        grad_weight,
        grad_features.reshape(row_count, width),
    )


def solution(mesh):
    rows = P(AXES, None)
    flat = P(AXES)
    tiles = P(AXES, None, None)
    in_specs = (rows, flat, flat, tiles, flat, flat, tiles, P(), rows)
    return jax.shard_map(
        body, mesh=mesh, in_specs=in_specs, out_specs=(rows, P(), rows), check_vma=False
    )
```

```python
import functools
import math

import jax
import jax.numpy as jnp
from jax import lax
from jax.experimental import pallas as pl
from jax.experimental.pallas import tpu as pltpu
from jax.sharding import PartitionSpec as P

BLOCK = 128
BLK_DEV = 16
AXES = ("group", "member")
VMEM = pl.BlockSpec(memory_space=pltpu.VMEM)
SMEM = pl.BlockSpec(memory_space=pltpu.SMEM)
MESH = pl.DeviceIdType.MESH
LIMIT = 56 * 1024 * 1024


def dot(a, b):
    return jnp.dot(a, b, preferred_element_type=jnp.float32)


def dot_lt(a, b):
    return lax.dot_general(a, b, (((0,), (0,)), ((), ())), preferred_element_type=jnp.float32)


def dot_rt(a, b):
    return lax.dot_general(a, b, (((1,), (1,)), ((), ())), preferred_element_type=jnp.float32)


def fill_terms(v, pair, home_r, tiles_r, send):
    @pl.loop(0, send.shape[0] // 4)
    def _(i):
        for j in range(4):
            k = i * 4 + j
            p = pair[k]
            send[k, BLOCK:] = dot_lt(tiles_r[p], v[home_r[p]]).astype(jnp.bfloat16)


def fill_blocks(v, asked, send):
    @pl.loop(0, send.shape[0] // 4)
    def _(i):
        for j in range(4):
            k = i * 4 + j
            send[k, :BLOCK] = v[jnp.maximum(asked[k], 0)]


def add_remote(acc, arrived, asked, home_r, target, tiles_r):
    @pl.loop(0, tiles_r.shape[0] // 4)
    def _(i):
        ps = [i * 4 + j for j in range(4)]
        terms = [dot(tiles_r[p], arrived[target[p], :BLOCK]) for p in ps]
        for p, term in zip(ps, terms):
            acc[home_r[p]] += term

    @pl.loop(0, arrived.shape[0])
    def _(j):
        @pl.when(asked[j] >= 0)
        def _():
            acc[asked[j]] += arrived[j, BLOCK:].astype(jnp.float32)


def place(index, members):
    return (index // members, lax.rem(index, members))


def send_kernel(members, home_r, pair, request, v, tiles_r, send, asked, came, seen, sent, got, local):
    devices = send.shape[0]
    me = lax.axis_index("group") * members + lax.axis_index("member")
    barrier = pltpu.get_barrier_semaphore()

    @pl.loop(1, devices)
    def _(k):
        pl.semaphore_signal(
            barrier, inc=1, device_id=place(lax.rem(me + k, devices), members), device_id_type=MESH
        )

    pl.semaphore_wait(barrier, devices - 1)

    def copy(k, slot):
        peer = lax.rem(me + k, devices)
        row = me if slot is None else peer
        return pltpu.make_async_remote_copy(
            src_ref=request,
            dst_ref=came.at[row],
            send_sem=sent.at[peer],
            recv_sem=got.at[row],
            device_id=place(peer, members),
            device_id_type=MESH,
        )

    @pl.loop(1, devices)
    def _(k):
        copy(k, None).start()

    came[me] = request[...]
    fill_terms(v, pair, home_r, tiles_r, send)

    @pl.loop(1, devices)
    def _(k):
        copy(k, 1).wait()

    down = pltpu.make_async_copy(came, seen, local)
    down.start()
    down.wait()

    @pl.loop(0, devices)
    def _(j):
        asked[j] = seen[j, 0, me]

    @pl.loop(0, devices // 4)
    def _(i):
        for j in range(4):
            k = i * 4 + j
            send[k, :BLOCK] = v[jnp.maximum(seen[k, 0, me], 0)]


def local_sums(home, near, v, tiles, acc):
    @pl.loop(0, tiles.shape[0], unroll=2)
    def _(p):
        h, n = home[p], near[p]
        tile = tiles[p]
        acc[h] += dot(tile, v[n])
        acc[n] += dot_lt(tile, v[h])


def first_kernel(home, near, v, tiles, acc):
    acc[...] = jnp.zeros_like(acc)
    local_sums(home, near, v, tiles, acc)


STEP = 4


def gates(f, a, c, weight):
    width = f.shape[-1]
    z = dot(f, weight[:width]) + dot(a, weight[width:])
    s = jax.nn.sigmoid(z)
    g = (c.astype(jnp.float32) * s * (1.0 + z * (1.0 - s))).astype(jnp.bfloat16)
    return z * s, g


def middle_kernel(
    asked, home_r, target, pair, arrived, local, tiles_r, feats, weight, cot, agg, grad_agg, send, acc
):
    width = feats.shape[-1]
    rows = STEP * BLOCK
    acc[...] = local[...]
    add_remote(acc, arrived, asked, home_r, target, tiles_r)

    @pl.loop(0, feats.shape[0] // STEP)
    def _(i):
        sl = pl.ds(i * STEP, STEP)
        flat = lambda ref: ref[sl].reshape(rows, width)
        a = flat(acc).astype(jnp.bfloat16)
        agg[sl] = a.reshape(STEP, BLOCK, width)
        _, g = gates(flat(feats), a, flat(cot), weight)
        grad_agg[sl] = dot_rt(g, weight[width:]).astype(jnp.bfloat16).reshape(STEP, BLOCK, width)

    fill_terms(grad_agg, pair, home_r, tiles_r, send)
    fill_blocks(grad_agg, asked, send)


def second_kernel(home, near, feats, agg, cot, weight, grad_agg, tiles, out, acc, partial):
    width = feats.shape[-1]
    half = partial.shape[-1]
    rows = STEP * BLOCK
    partial[...] = jnp.zeros_like(partial)

    @pl.loop(0, feats.shape[0] // STEP)
    def _(i):
        sl = pl.ds(i * STEP, STEP)
        flat = lambda ref: ref[sl].reshape(rows, width)
        f, a = flat(feats), flat(agg)
        o, g = gates(f, a, flat(cot), weight)
        out[sl] = o.astype(jnp.bfloat16).reshape(STEP, BLOCK, width)
        for part in range(2):
            cols = g[:, part * half : (part + 1) * half]
            partial[part, :width] += dot_lt(f, cols)
            partial[part, width:] += dot_lt(a, cols)
        acc[sl] = dot_rt(g, weight[:width]).reshape(STEP, BLOCK, width)

    local_sums(home, near, grad_agg, tiles, acc)


def reduce_kernel(members, x, res, acc, came, send_sem, recv_sem):
    g, m = lax.axis_index("group"), lax.axis_index("member")
    bits = members.bit_length() - 1
    peers, sides = [(1 - g, m)], []
    for b in range(bits):
        side = lax.rem(m // (1 << b), 2)
        sides.append(side)
        peers.append((g, m + (1 - 2 * side) * (1 << b)))
    barrier = pltpu.get_barrier_semaphore()
    for peer in peers:
        pl.semaphore_signal(barrier, inc=1, device_id=peer, device_id_type=MESH)
    pl.semaphore_wait(barrier, bits + 1)

    def trade(src, dst, sem, peer):
        copy = pltpu.make_async_remote_copy(
            src_ref=src,
            dst_ref=dst,
            send_sem=send_sem.at[sem],
            recv_sem=recv_sem.at[sem],
            device_id=peer,
            device_id_type=MESH,
        )
        copy.start()
        copy.wait()

    total = x.shape[1]
    trade(x.at[1 - g], came.at[pl.ds(0, total)], 0, peers[0])
    acc[...] = x[g] + came[:total]
    low, size, spot, lows = 0, total, total, []
    for b in range(bits):
        lows.append(low)
        size //= 2
        give = pl.multiple_of(low + (1 - sides[b]) * size, 8)
        keep = pl.multiple_of(low + sides[b] * size, 8)
        trade(acc.at[pl.ds(give, size)], came.at[pl.ds(spot, size)], 1 + b, peers[1 + b])
        acc[pl.ds(keep, size)] += came[spot : spot + size]
        low, spot = keep, spot + size
    res[g, pl.ds(low, size)] = acc[pl.ds(low, size)]
    for b in reversed(range(bits)):
        region = res.at[g, pl.ds(low, size)]
        trade(region, region, 1 + bits + b, peers[1 + b])
        low, size = lows[b], size * 2
    trade(res.at[g], res.at[g], 1 + 2 * bits, peers[0])


def final_kernel(asked, home_r, target, arrived, local, tiles_r, out):
    out[...] = local[...]
    add_remote(out, arrived, asked, home_r, target, tiles_r)


def call(kernel, out_shape, n_smem, n_vmem, scratch=(), flops=0, moved=0, out_specs=None, cid=None):
    params = dict(vmem_limit_bytes=LIMIT)
    if cid is not None:
        params.update(collective_id=cid, has_side_effects=True)
    return pl.pallas_call(
        kernel,
        out_shape=out_shape,
        in_specs=[SMEM] * n_smem + [VMEM] * n_vmem,
        out_specs=jax.tree.map(lambda _: VMEM, out_shape) if out_specs is None else out_specs,
        scratch_shapes=list(scratch),
        compiler_params=pltpu.CompilerParams(**params),
        cost_estimate=pl.CostEstimate(flops=flops, bytes_accessed=moved, transcendentals=0),
    )


def exchange(buffer):
    return lax.all_to_all(buffer, AXES, split_axis=0, concat_axis=0, tiled=True)


def body(
    features, local_home, local_near, local_tiles, remote_home, remote_far, remote_tiles, weight, cotangent
):
    devices = lax.axis_size(AXES)
    row_count, width = features.shape
    blocks = row_count // BLOCK
    bf16, f32 = jnp.bfloat16, jnp.float32
    shaped = lambda dtype: jax.ShapeDtypeStruct((blocks, BLOCK, width), dtype)
    send_shape = jax.ShapeDtypeStruct((devices, 2 * BLOCK, width), bf16)
    target = remote_far // BLK_DEV
    pairs = remote_far.shape[0]
    members = devices // lax.axis_size("group")
    hit = target[None, :] == jnp.arange(devices, dtype=jnp.int32)[:, None]
    pair = jnp.sum(jnp.where(hit, jnp.arange(pairs, dtype=jnp.int32)[None, :], 0), axis=1)
    lanes = -(-devices // 128) * 128
    row_hit = target[None, :] == jnp.arange(lanes, dtype=jnp.int32)[:, None]
    request = jnp.sum(jnp.where(row_hit, (remote_far % BLK_DEV + 1)[None, :], 0), axis=1)[None, :] - 1
    feats = features.reshape(blocks, BLOCK, width)
    cot = cotangent.reshape(blocks, BLOCK, width)
    local_flops = 4 * BLOCK * BLOCK * width * local_tiles.shape[0]
    dma = pltpu.SemaphoreType.DMA

    send1, asked = call(
        functools.partial(send_kernel, members),
        (send_shape, jax.ShapeDtypeStruct((devices,), jnp.int32)),
        2,
        3,
        scratch=[
            pltpu.VMEM((devices, 1, lanes), jnp.int32),
            pltpu.SMEM((devices, 1, lanes), jnp.int32),
            dma((devices,)),
            dma((devices,)),
            dma(()),
        ],
        out_specs=(VMEM, SMEM),
        cid=0,
    )(remote_home, pair, request, feats, remote_tiles)
    idx = (asked, remote_home, target)
    arrived1 = exchange(send1)
    local1 = call(first_kernel, shaped(f32), 2, 2, flops=20 * local_flops, moved=20 << 20)(
        local_home, local_near, feats, local_tiles
    )
    agg, grad_agg, send2 = call(
        middle_kernel,
        (shaped(bf16), shaped(bf16), send_shape),
        4,
        6,
        scratch=[pltpu.VMEM((blocks, BLOCK, width), f32)],
    )(*idx, pair, arrived1, local1, remote_tiles, feats, weight, cot)
    arrived2 = exchange(send2)
    part = jax.ShapeDtypeStruct((2, weight.shape[0], width // 2), f32)
    out, local2, partial = call(
        second_kernel, (shaped(bf16), shaped(f32), part), 2, 6, flops=20 * local_flops, moved=20 << 20
    )(local_home, local_near, feats, agg, cot, weight, grad_agg, local_tiles)
    steps = 2 * members.bit_length()
    summed = call(
        functools.partial(reduce_kernel, members),
        part,
        0,
        1,
        scratch=[
            pltpu.VMEM(part.shape[1:], f32),
            pltpu.VMEM((2 * part.shape[1], part.shape[2]), f32),
            dma((steps,)),
            dma((steps,)),
        ],
        flops=20 * local_flops,
        moved=20 << 20,
        cid=1,
    )(partial)
    grad_scale = 1.0 / math.sqrt(row_count * devices)
    grad_weight = jnp.concatenate([summed[0], summed[1]], axis=1) * grad_scale
    grad_features = call(final_kernel, shaped(f32), 3, 3)(*idx, arrived2, local2, remote_tiles)
    return (
        out.reshape(row_count, width),
        grad_weight,
        grad_features.reshape(row_count, width),
    )


def solution(mesh):
    rows = P(AXES, None)
    flat = P(AXES)
    tiles = P(AXES, None, None)
    in_specs = (rows, flat, flat, tiles, flat, flat, tiles, P(), rows)
    return jax.shard_map(
        body, mesh=mesh, in_specs=in_specs, out_specs=(rows, P(), rows), check_vma=False
    )
```

```python
import functools
import math

import jax
import jax.numpy as jnp
from jax import lax
from jax.experimental import pallas as pl
from jax.experimental.pallas import tpu as pltpu
from jax.sharding import PartitionSpec as P

BLOCK = 128
BLK_DEV = 16
AXES = ("group", "member")
VMEM = pl.BlockSpec(memory_space=pltpu.VMEM)
SMEM = pl.BlockSpec(memory_space=pltpu.SMEM)
MESH = pl.DeviceIdType.MESH
HBM = pl.BlockSpec(memory_space=pl.ANY)
LIMIT = 56 * 1024 * 1024


def dot(a, b):
    return jnp.dot(a, b, preferred_element_type=jnp.float32)


def dot_lt(a, b):
    return lax.dot_general(a, b, (((0,), (0,)), ((), ())), preferred_element_type=jnp.float32)


def dot_rt(a, b):
    return lax.dot_general(a, b, (((1,), (1,)), ((), ())), preferred_element_type=jnp.float32)


def fill_terms(v, pair, home_r, tiles_r, send):
    @pl.loop(0, send.shape[0] // 4)
    def _(i):
        for j in range(4):
            k = i * 4 + j
            p = pair[k]
            send[k, send.shape[1] - BLOCK :] = dot_lt(tiles_r[p], v[home_r[p]]).astype(jnp.bfloat16)


def fill_blocks(v, asked, send):
    @pl.loop(0, send.shape[0] // 4)
    def _(i):
        for j in range(4):
            k = i * 4 + j
            send[k, :BLOCK] = v[jnp.maximum(asked[k], 0)]


def add_remote(acc, came, terms_in, asked, home_r, target, tiles_r):
    first = terms_in.shape[1] - BLOCK

    @pl.loop(0, tiles_r.shape[0] // 4)
    def _(i):
        ps = [i * 4 + j for j in range(4)]
        terms = [dot(tiles_r[p], came[target[p], :BLOCK]) for p in ps]
        for p, term in zip(ps, terms):
            acc[home_r[p]] += term

    @pl.loop(0, terms_in.shape[0])
    def _(j):
        @pl.when(asked[j] >= 0)
        def _():
            acc[asked[j]] += terms_in[j, first:].astype(jnp.float32)


def place(index, members):
    return (index // members, lax.rem(index, members))


def send_kernel(members, home_r, pair, request, v, tiles_r, send, asked, came, seen, sent, got, local):
    devices = send.shape[0]
    me = lax.axis_index("group") * members + lax.axis_index("member")
    barrier = pltpu.get_barrier_semaphore()

    @pl.loop(1, devices)
    def _(k):
        pl.semaphore_signal(
            barrier, inc=1, device_id=place(lax.rem(me + k, devices), members), device_id_type=MESH
        )

    pl.semaphore_wait(barrier, devices - 1)

    def copy(k, slot):
        peer = lax.rem(me + k, devices)
        row = me if slot is None else peer
        return pltpu.make_async_remote_copy(
            src_ref=request,
            dst_ref=came.at[row],
            send_sem=sent.at[peer],
            recv_sem=got.at[row],
            device_id=place(peer, members),
            device_id_type=MESH,
        )

    @pl.loop(1, devices)
    def _(k):
        copy(k, None).start()

    came[me] = request[...]
    fill_terms(v, pair, home_r, tiles_r, send)

    @pl.loop(1, devices)
    def _(k):
        copy(k, 1).wait()

    down = pltpu.make_async_copy(came, seen, local)
    down.start()
    down.wait()

    @pl.loop(0, devices)
    def _(j):
        asked[j] = seen[j, 0, me]

    @pl.loop(0, devices // 4)
    def _(i):
        for j in range(4):
            k = i * 4 + j
            send[k, :BLOCK] = v[jnp.maximum(seen[k, 0, me], 0)]


def local_sums(home, near, v, tiles, acc):
    @pl.loop(0, tiles.shape[0], unroll=2)
    def _(p):
        h, n = home[p], near[p]
        tile = tiles[p]
        acc[h] += dot(tile, v[n])
        acc[n] += dot_lt(tile, v[h])


def first_kernel(home, near, v, tiles, acc):
    acc[...] = jnp.zeros_like(acc)
    local_sums(home, near, v, tiles, acc)


STEP = 4


def gates(f, a, c, weight):
    width = f.shape[-1]
    z = dot(f, weight[:width]) + dot(a, weight[width:])
    s = jax.nn.sigmoid(z)
    g = (c.astype(jnp.float32) * s * (1.0 + z * (1.0 - s))).astype(jnp.bfloat16)
    return z * s, g


def middle_kernel(
    asked, home_r, target, pair, arrived, local, tiles_r, feats, weight, cot, agg, grad_agg, send, acc
):
    width = feats.shape[-1]
    rows = STEP * BLOCK
    acc[...] = local[...]
    add_remote(acc, arrived, arrived, asked, home_r, target, tiles_r)

    @pl.loop(0, feats.shape[0] // STEP)
    def _(i):
        sl = pl.ds(i * STEP, STEP)
        flat = lambda ref: ref[sl].reshape(rows, width)
        a = flat(acc).astype(jnp.bfloat16)
        agg[sl] = a.reshape(STEP, BLOCK, width)
        _, g = gates(flat(feats), a, flat(cot), weight)
        grad_agg[sl] = dot_rt(g, weight[width:]).astype(jnp.bfloat16).reshape(STEP, BLOCK, width)

    fill_terms(grad_agg, pair, home_r, tiles_r, send)


def second_kernel(home, near, asked, feats, agg, cot, weight, grad_agg, tiles, out, acc, partial, send):
    width = feats.shape[-1]
    half = partial.shape[-1]
    rows = STEP * BLOCK
    fill_blocks(grad_agg, asked, send)
    partial[...] = jnp.zeros_like(partial)

    @pl.loop(0, feats.shape[0] // STEP)
    def _(i):
        sl = pl.ds(i * STEP, STEP)
        flat = lambda ref: ref[sl].reshape(rows, width)
        f, a = flat(feats), flat(agg)
        o, g = gates(f, a, flat(cot), weight)
        out[sl] = o.astype(jnp.bfloat16).reshape(STEP, BLOCK, width)
        for part in range(2):
            cols = g[:, part * half : (part + 1) * half]
            partial[part, :width] += dot_lt(f, cols)
            partial[part, width:] += dot_lt(a, cols)
        acc[sl] = dot_rt(g, weight[:width]).reshape(STEP, BLOCK, width)

    local_sums(home, near, grad_agg, tiles, acc)


def reduce_kernel(
    members, x, blocks, res, arrived, acc, came, send_sem, recv_sem, sent, got
):
    devices = blocks.shape[0]
    g, m = lax.axis_index("group"), lax.axis_index("member")
    me = g * members + m
    bits = members.bit_length() - 1
    peers, sides = [(1 - g, m)], []
    for b in range(bits):
        side = lax.rem(m // (1 << b), 2)
        sides.append(side)
        peers.append((g, m + (1 - 2 * side) * (1 << b)))
    barrier = pltpu.get_barrier_semaphore()

    @pl.loop(1, devices)
    def _(k):
        pl.semaphore_signal(
            barrier, inc=1, device_id=place(lax.rem(me + k, devices), members), device_id_type=MESH
        )

    pl.semaphore_wait(barrier, devices - 1)

    def block_copy(k, arriving):
        peer = lax.rem(me + k, devices)
        row = peer if arriving else me
        return pltpu.make_async_remote_copy(
            src_ref=blocks.at[peer],
            dst_ref=arrived.at[row],
            send_sem=sent.at[peer],
            recv_sem=got.at[row],
            device_id=place(peer, members),
            device_id_type=MESH,
        )

    trades = 2 * bits + 2
    share = -(-(devices - 1) // trades)

    def trade(src, dst, sem, peer):
        copy = pltpu.make_async_remote_copy(
            src_ref=src,
            dst_ref=dst,
            send_sem=send_sem.at[sem],
            recv_sem=recv_sem.at[sem],
            device_id=peer,
            device_id_type=MESH,
        )
        copy.start()
        first = 1 + sem * share

        @pl.loop(min(first, devices), min(first + share, devices))
        def _(k):
            block_copy(k, False).start()

        copy.wait()

    total = x.shape[1]
    trade(x.at[1 - g], came.at[pl.ds(0, total)], 0, peers[0])
    acc[...] = x[g] + came[:total]
    low, size, spot, lows = 0, total, total, []
    for b in range(bits):
        lows.append(low)
        size //= 2
        give = pl.multiple_of(low + (1 - sides[b]) * size, 8)
        keep = pl.multiple_of(low + sides[b] * size, 8)
        trade(acc.at[pl.ds(give, size)], came.at[pl.ds(spot, size)], 1 + b, peers[1 + b])
        acc[pl.ds(keep, size)] += came[spot : spot + size]
        low, spot = keep, spot + size
    res[g, pl.ds(low, size)] = acc[pl.ds(low, size)]
    for b in reversed(range(bits)):
        region = res.at[g, pl.ds(low, size)]
        trade(region, region, 2 * bits - b, peers[1 + b])
        low, size = lows[b], size * 2
    trade(res.at[g], res.at[g], 1 + 2 * bits, peers[0])

    @pl.loop(1, devices)
    def _(k):
        block_copy(k, True).wait()


def final_kernel(asked, home_r, target, blocks, terms, local, tiles_r, out):
    out[...] = local[...]
    add_remote(out, blocks, terms, asked, home_r, target, tiles_r)


def call(kernel, out_shape, n_smem, n_vmem, scratch=(), flops=0, moved=0, out_specs=None, in_specs=None, cid=None):
    params = dict(vmem_limit_bytes=LIMIT)
    if cid is not None:
        params.update(collective_id=cid, has_side_effects=True)
    return pl.pallas_call(
        kernel,
        out_shape=out_shape,
        in_specs=in_specs or [SMEM] * n_smem + [VMEM] * n_vmem,
        out_specs=jax.tree.map(lambda _: VMEM, out_shape) if out_specs is None else out_specs,
        scratch_shapes=list(scratch),
        compiler_params=pltpu.CompilerParams(**params),
        cost_estimate=pl.CostEstimate(flops=flops, bytes_accessed=moved, transcendentals=0),
    )


def exchange(buffer):
    return lax.all_to_all(buffer, AXES, split_axis=0, concat_axis=0, tiled=True)


def body(
    features, local_home, local_near, local_tiles, remote_home, remote_far, remote_tiles, weight, cotangent
):
    devices = lax.axis_size(AXES)
    row_count, width = features.shape
    blocks = row_count // BLOCK
    bf16, f32 = jnp.bfloat16, jnp.float32
    shaped = lambda dtype: jax.ShapeDtypeStruct((blocks, BLOCK, width), dtype)
    send_shape = jax.ShapeDtypeStruct((devices, 2 * BLOCK, width), bf16)
    half_shape = jax.ShapeDtypeStruct((devices, BLOCK, width), bf16)
    target = remote_far // BLK_DEV
    pairs = remote_far.shape[0]
    members = devices // lax.axis_size("group")
    hit = target[None, :] == jnp.arange(devices, dtype=jnp.int32)[:, None]
    pair = jnp.sum(jnp.where(hit, jnp.arange(pairs, dtype=jnp.int32)[None, :], 0), axis=1)
    lanes = -(-devices // 128) * 128
    row_hit = target[None, :] == jnp.arange(lanes, dtype=jnp.int32)[:, None]
    request = jnp.sum(jnp.where(row_hit, (remote_far % BLK_DEV + 1)[None, :], 0), axis=1)[None, :] - 1
    feats = features.reshape(blocks, BLOCK, width)
    cot = cotangent.reshape(blocks, BLOCK, width)
    local_flops = 4 * BLOCK * BLOCK * width * local_tiles.shape[0]
    dma = pltpu.SemaphoreType.DMA

    send1, asked = call(
        functools.partial(send_kernel, members),
        (send_shape, jax.ShapeDtypeStruct((devices,), jnp.int32)),
        2,
        3,
        scratch=[
            pltpu.VMEM((devices, 1, lanes), jnp.int32),
            pltpu.SMEM((devices, 1, lanes), jnp.int32),
            dma((devices,)),
            dma((devices,)),
            dma(()),
        ],
        out_specs=(VMEM, SMEM),
        cid=0,
    )(remote_home, pair, request, feats, remote_tiles)
    idx = (asked, remote_home, target)
    arrived1 = exchange(send1)
    local1 = call(first_kernel, shaped(f32), 2, 2, flops=20 * local_flops, moved=20 << 20)(
        local_home, local_near, feats, local_tiles
    )
    agg, grad_agg, send2 = call(
        middle_kernel,
        (shaped(bf16), shaped(bf16), half_shape),
        4,
        6,
        scratch=[pltpu.VMEM((blocks, BLOCK, width), f32)],
    )(*idx, pair, arrived1, local1, remote_tiles, feats, weight, cot)
    terms2 = exchange(send2)
    part = jax.ShapeDtypeStruct((2, weight.shape[0], width // 2), f32)
    out, local2, partial, send3 = call(
        second_kernel,
        (shaped(bf16), shaped(f32), part, half_shape),
        3,
        6,
        flops=20 * local_flops,
        moved=20 << 20,
    )(local_home, local_near, asked, feats, agg, cot, weight, grad_agg, local_tiles)
    steps = 2 * members.bit_length()
    summed, blocks2 = call(
        functools.partial(reduce_kernel, members),
        (part, half_shape),
        0,
        2,
        scratch=[
            pltpu.VMEM(part.shape[1:], f32),
            pltpu.VMEM((2 * part.shape[1], part.shape[2]), f32),
            dma((steps,)),
            dma((steps,)),
            dma((devices,)),
            dma((devices,)),
        ],
        flops=20 * local_flops,
        moved=20 << 20,
        in_specs=[VMEM, HBM],
        out_specs=(VMEM, HBM),
        cid=1,
    )(partial, send3)
    grad_scale = 1.0 / math.sqrt(row_count * devices)
    grad_weight = jnp.concatenate([summed[0], summed[1]], axis=1) * grad_scale
    grad_features = call(final_kernel, shaped(f32), 3, 4)(
        *idx, blocks2, terms2, local2, remote_tiles
    )
    return (
        out.reshape(row_count, width),
        grad_weight,
        grad_features.reshape(row_count, width),
    )


def solution(mesh):
    rows = P(AXES, None)
    flat = P(AXES)
    tiles = P(AXES, None, None)
    in_specs = (rows, flat, flat, tiles, flat, flat, tiles, P(), rows)
    return jax.shard_map(
        body, mesh=mesh, in_specs=in_specs, out_specs=(rows, P(), rows), check_vma=False
    )
```

```python
import functools
import math

import jax
import jax.numpy as jnp
from jax import lax
from jax.experimental import pallas as pl
from jax.experimental.pallas import tpu as pltpu
from jax.sharding import PartitionSpec as P

BLOCK = 128
BLK_DEV = 16
AXES = ("group", "member")
VMEM = pl.BlockSpec(memory_space=pltpu.VMEM)
SMEM = pl.BlockSpec(memory_space=pltpu.SMEM)
MESH = pl.DeviceIdType.MESH
HBM = pl.BlockSpec(memory_space=pl.ANY)
LIMIT = 63 * 1024 * 1024


def dot(a, b):
    return jnp.dot(a, b, preferred_element_type=jnp.float32)


def dot_lt(a, b):
    return lax.dot_general(a, b, (((0,), (0,)), ((), ())), preferred_element_type=jnp.float32)


def dot_rt(a, b):
    return lax.dot_general(a, b, (((1,), (1,)), ((), ())), preferred_element_type=jnp.float32)


def fill_terms(v, pair, home_r, tiles_r, send, part=0, parts=1):
    count = send.shape[0] // 4 // parts

    @pl.loop(part * count, (part + 1) * count)
    def _(i):
        for j in range(4):
            k = i * 4 + j
            p = pair[k]
            send[k, send.shape[1] - BLOCK :] = dot_lt(tiles_r[p], v[home_r[p]]).astype(jnp.bfloat16)


def fill_blocks(v, asked, send):
    @pl.loop(0, send.shape[0] // 4)
    def _(i):
        for j in range(4):
            k = i * 4 + j
            send[k, :BLOCK] = v[jnp.maximum(asked[k], 0)]


def add_products(acc, came, home_r, target, tiles_r):
    @pl.loop(0, tiles_r.shape[0] // 4)
    def _(i):
        ps = [i * 4 + j for j in range(4)]
        terms = [dot(tiles_r[p], came[target[p], :BLOCK]) for p in ps]
        for p, term in zip(ps, terms):
            acc[home_r[p]] += term


def add_terms(acc, came, asked):
    first = came.shape[1] - BLOCK

    @pl.loop(0, came.shape[0])
    def _(j):
        @pl.when(asked[j] >= 0)
        def _():
            acc[asked[j]] += came[j, first:].astype(jnp.float32)


def begin(src, dst, sems, i):
    copy = pltpu.make_async_copy(src, dst, sems.at[i])
    copy.start()
    return copy


def place(index, members):
    return (index // members, lax.rem(index, members))


def send_kernel(members, home_r, pair, request, v, tiles_r, send, asked, came, seen, sent, got, local):
    devices = send.shape[0]
    me = lax.axis_index("group") * members + lax.axis_index("member")
    barrier = pltpu.get_barrier_semaphore()

    @pl.loop(1, devices)
    def _(k):
        pl.semaphore_signal(
            barrier, inc=1, device_id=place(lax.rem(me + k, devices), members), device_id_type=MESH
        )

    fill_terms(v, pair, home_r, tiles_r, send, 0, 2)
    pl.semaphore_wait(barrier, devices - 1)

    def copy(k, slot):
        peer = lax.rem(me + k, devices)
        row = me if slot is None else peer
        return pltpu.make_async_remote_copy(
            src_ref=request,
            dst_ref=came.at[row],
            send_sem=sent.at[peer],
            recv_sem=got.at[row],
            device_id=place(peer, members),
            device_id_type=MESH,
        )

    @pl.loop(1, devices)
    def _(k):
        copy(k, None).start()

    came[me] = request[...]
    fill_terms(v, pair, home_r, tiles_r, send, 1, 2)

    @pl.loop(1, devices)
    def _(k):
        copy(k, 1).wait()

    down = pltpu.make_async_copy(came, seen, local)
    down.start()
    down.wait()

    @pl.loop(0, devices)
    def _(j):
        asked[j] = seen[j, 0, me]

    @pl.loop(0, devices // 4)
    def _(i):
        for j in range(4):
            k = i * 4 + j
            send[k, :BLOCK] = v[jnp.maximum(seen[k, 0, me], 0)]


def local_sums(home, near, v, tiles, acc):
    @pl.loop(0, tiles.shape[0], unroll=2)
    def _(p):
        h, n = home[p], near[p]
        tile = tiles[p]
        acc[h] += dot(tile, v[n])
        acc[n] += dot_lt(tile, v[h])


def first_kernel(home, near, v, tiles, acc):
    acc[...] = jnp.zeros_like(acc)
    local_sums(home, near, v, tiles, acc)


STEP = 4


def gates(f, a, c, weight):
    width = f.shape[-1]
    z = dot(f, weight[:width]) + dot(a, weight[width:])
    s = jax.nn.sigmoid(z)
    g = (c.astype(jnp.float32) * s * (1.0 + z * (1.0 - s))).astype(jnp.bfloat16)
    return z * s, g


PARTS = 4


def middle_kernel(
    asked, home_r, target, pair, arrived_h, local_h, feats_h, cot_h, tiles_r, weight,
    agg_h, grad_agg_h, send_h, arrived, acc, feats, cot, agg, grad_agg, send, sems,
):
    copies = [
        begin(src, dst, sems, i)
        for i, (src, dst) in enumerate(
            [(arrived_h, arrived), (local_h, acc), (feats_h, feats), (cot_h, cot)]
        )
    ]
    width = feats.shape[-1]
    rows = STEP * BLOCK
    copies[0].wait()
    copies[1].wait()
    add_products(acc, arrived, home_r, target, tiles_r)
    add_terms(acc, arrived, asked)
    copies[2].wait()
    copies[3].wait()

    @pl.loop(0, feats.shape[0] // STEP)
    def _(i):
        sl = pl.ds(i * STEP, STEP)
        flat = lambda ref: ref[sl].reshape(rows, width)
        a = flat(acc).astype(jnp.bfloat16)
        agg[sl] = a.reshape(STEP, BLOCK, width)
        _, g = gates(flat(feats), a, flat(cot), weight)
        grad_agg[sl] = dot_rt(g, weight[width:]).astype(jnp.bfloat16).reshape(STEP, BLOCK, width)

    copies = [begin(agg, agg_h, sems, 4), begin(grad_agg, grad_agg_h, sems, 5)]
    size = send.shape[0] // PARTS
    for part in range(PARTS):
        fill_terms(grad_agg, pair, home_r, tiles_r, send, part, PARTS)
        sl = pl.ds(part * size, size)
        copies.append(begin(send.at[sl], send_h.at[sl], sems, 6 + part))
    for copy in copies:
        copy.wait()


def second_kernel(home, near, asked, feats, agg, cot, weight, grad_agg, tiles, out, acc, partial, send):
    width = feats.shape[-1]
    half = partial.shape[-1]
    rows = STEP * BLOCK
    fill_blocks(grad_agg, asked, send)
    partial[...] = jnp.zeros_like(partial)

    @pl.loop(0, feats.shape[0] // STEP)
    def _(i):
        sl = pl.ds(i * STEP, STEP)
        flat = lambda ref: ref[sl].reshape(rows, width)
        f, a = flat(feats), flat(agg)
        o, g = gates(f, a, flat(cot), weight)
        out[sl] = o.astype(jnp.bfloat16).reshape(STEP, BLOCK, width)
        for part in range(2):
            cols = g[:, part * half : (part + 1) * half]
            partial[part, :width] += dot_lt(f, cols)
            partial[part, width:] += dot_lt(a, cols)
        acc[sl] = dot_rt(g, weight[:width]).reshape(STEP, BLOCK, width)

    local_sums(home, near, grad_agg, tiles, acc)


def reduce_kernel(
    members, x, blocks, res, arrived, acc, came, send_sem, recv_sem, sent, got
):
    devices = blocks.shape[0]
    g, m = lax.axis_index("group"), lax.axis_index("member")
    me = g * members + m
    bits = members.bit_length() - 1
    peers, sides = [(1 - g, m)], []
    for b in range(bits):
        side = lax.rem(m // (1 << b), 2)
        sides.append(side)
        peers.append((g, m + (1 - 2 * side) * (1 << b)))
    barrier = pltpu.get_barrier_semaphore()

    @pl.loop(1, devices)
    def _(k):
        pl.semaphore_signal(
            barrier, inc=1, device_id=place(lax.rem(me + k, devices), members), device_id_type=MESH
        )

    pl.semaphore_wait(barrier, devices - 1)

    def block_copy(k, arriving):
        peer = lax.rem(me + k, devices)
        row = peer if arriving else me
        return pltpu.make_async_remote_copy(
            src_ref=blocks.at[peer],
            dst_ref=arrived.at[row],
            send_sem=sent.at[peer],
            recv_sem=got.at[row],
            device_id=place(peer, members),
            device_id_type=MESH,
        )

    trades = 2 * bits + 2
    share = -(-(devices - 1) // trades)

    def trade(src, dst, sem, peer):
        copy = pltpu.make_async_remote_copy(
            src_ref=src,
            dst_ref=dst,
            send_sem=send_sem.at[sem],
            recv_sem=recv_sem.at[sem],
            device_id=peer,
            device_id_type=MESH,
        )
        copy.start()
        first = 1 + sem * share

        @pl.loop(min(first, devices), min(first + share, devices))
        def _(k):
            block_copy(k, False).start()

        copy.wait()

    total = x.shape[1]
    trade(x.at[1 - g], came.at[pl.ds(0, total)], 0, peers[0])
    acc[...] = x[g] + came[:total]
    low, size, spot, lows = 0, total, total, []
    for b in range(bits):
        lows.append(low)
        size //= 2
        give = pl.multiple_of(low + (1 - sides[b]) * size, 8)
        keep = pl.multiple_of(low + sides[b] * size, 8)
        trade(acc.at[pl.ds(give, size)], came.at[pl.ds(spot, size)], 1 + b, peers[1 + b])
        acc[pl.ds(keep, size)] += came[spot : spot + size]
        low, spot = keep, spot + size
    res[g, pl.ds(low, size)] = acc[pl.ds(low, size)]
    for b in reversed(range(bits)):
        region = res.at[g, pl.ds(low, size)]
        trade(region, region, 2 * bits - b, peers[1 + b])
        low, size = lows[b], size * 2
    trade(res.at[g], res.at[g], 1 + 2 * bits, peers[0])

    @pl.loop(1, devices)
    def _(k):
        block_copy(k, True).wait()


def final_kernel(
    asked, home_r, target, blocks_h, local_h, terms_h, tiles_r, out_h, blocks, terms, acc, sems
):
    copies = [
        begin(src, dst, sems, i)
        for i, (src, dst) in enumerate([(blocks_h, blocks), (local_h, acc), (terms_h, terms)])
    ]
    copies[0].wait()
    copies[1].wait()
    add_products(acc, blocks, home_r, target, tiles_r)
    copies[2].wait()
    add_terms(acc, terms, asked)
    begin(acc, out_h, sems, 3).wait()


def call(kernel, out_shape, n_smem, n_vmem, scratch=(), flops=0, moved=0, out_specs=None, in_specs=None, cid=None):
    params = dict(vmem_limit_bytes=LIMIT)
    if cid is not None:
        params.update(collective_id=cid, has_side_effects=True)
    return pl.pallas_call(
        kernel,
        out_shape=out_shape,
        in_specs=in_specs or [SMEM] * n_smem + [VMEM] * n_vmem,
        out_specs=jax.tree.map(lambda _: VMEM, out_shape) if out_specs is None else out_specs,
        scratch_shapes=list(scratch),
        compiler_params=pltpu.CompilerParams(**params),
        cost_estimate=pl.CostEstimate(flops=flops, bytes_accessed=moved, transcendentals=0),
    )


def exchange(buffer):
    return lax.all_to_all(buffer, AXES, split_axis=0, concat_axis=0, tiled=True)


def body(
    features, local_home, local_near, local_tiles, remote_home, remote_far, remote_tiles, weight, cotangent
):
    devices = lax.axis_size(AXES)
    row_count, width = features.shape
    blocks = row_count // BLOCK
    bf16, f32 = jnp.bfloat16, jnp.float32
    shaped = lambda dtype: jax.ShapeDtypeStruct((blocks, BLOCK, width), dtype)
    send_shape = jax.ShapeDtypeStruct((devices, 2 * BLOCK, width), bf16)
    half_shape = jax.ShapeDtypeStruct((devices, BLOCK, width), bf16)
    target = remote_far // BLK_DEV
    pairs = remote_far.shape[0]
    members = devices // lax.axis_size("group")
    hit = target[None, :] == jnp.arange(devices, dtype=jnp.int32)[:, None]
    pair = jnp.sum(jnp.where(hit, jnp.arange(pairs, dtype=jnp.int32)[None, :], 0), axis=1)
    lanes = -(-devices // 128) * 128
    row_hit = target[None, :] == jnp.arange(lanes, dtype=jnp.int32)[:, None]
    request = jnp.sum(jnp.where(row_hit, (remote_far % BLK_DEV + 1)[None, :], 0), axis=1)[None, :] - 1
    feats = features.reshape(blocks, BLOCK, width)
    cot = cotangent.reshape(blocks, BLOCK, width)
    local_flops = 4 * BLOCK * BLOCK * width * local_tiles.shape[0]
    dma = pltpu.SemaphoreType.DMA

    send1, asked = call(
        functools.partial(send_kernel, members),
        (send_shape, jax.ShapeDtypeStruct((devices,), jnp.int32)),
        2,
        3,
        scratch=[
            pltpu.VMEM((devices, 1, lanes), jnp.int32),
            pltpu.SMEM((devices, 1, lanes), jnp.int32),
            dma((devices,)),
            dma((devices,)),
            dma(()),
        ],
        out_specs=(VMEM, SMEM),
        cid=0,
    )(remote_home, pair, request, feats, remote_tiles)
    idx = (asked, remote_home, target)
    arrived1 = exchange(send1)
    local1 = call(first_kernel, shaped(f32), 2, 2, flops=20 * local_flops, moved=20 << 20)(
        local_home, local_near, feats, local_tiles
    )
    field = lambda dtype: pltpu.VMEM((blocks, BLOCK, width), dtype)
    agg, grad_agg, send2 = call(
        middle_kernel,
        (shaped(bf16), shaped(bf16), half_shape),
        4,
        6,
        scratch=[pltpu.VMEM(send_shape.shape, bf16), field(f32)]
        + [field(bf16)] * 4
        + [pltpu.VMEM(half_shape.shape, bf16), dma((6 + PARTS,))],
        in_specs=[SMEM] * 4 + [HBM] * 4 + [VMEM] * 2,
        out_specs=(HBM,) * 3,
    )(*idx, pair, arrived1, local1, feats, cot, remote_tiles, weight)
    terms2 = exchange(send2)
    part = jax.ShapeDtypeStruct((2, weight.shape[0], width // 2), f32)
    out, local2, partial, send3 = call(
        second_kernel,
        (shaped(bf16), shaped(f32), part, half_shape),
        3,
        6,
        flops=20 * local_flops,
        moved=20 << 20,
    )(local_home, local_near, asked, feats, agg, cot, weight, grad_agg, local_tiles)
    steps = 2 * members.bit_length()
    summed, blocks2 = call(
        functools.partial(reduce_kernel, members),
        (part, half_shape),
        0,
        2,
        scratch=[
            pltpu.VMEM(part.shape[1:], f32),
            pltpu.VMEM((2 * part.shape[1], part.shape[2]), f32),
            dma((steps,)),
            dma((steps,)),
            dma((devices,)),
            dma((devices,)),
        ],
        flops=20 * local_flops,
        moved=20 << 20,
        in_specs=[VMEM, HBM],
        out_specs=(VMEM, HBM),
        cid=1,
    )(partial, send3)
    grad_scale = 1.0 / math.sqrt(row_count * devices)
    grad_weight = jnp.concatenate([summed[0], summed[1]], axis=1) * grad_scale
    grad_features = call(
        final_kernel,
        shaped(f32),
        3,
        4,
        scratch=[pltpu.VMEM(half_shape.shape, bf16)] * 2 + [field(f32), dma((4,))],
        in_specs=[SMEM] * 3 + [HBM] * 3 + [VMEM],
        out_specs=HBM,
    )(*idx, blocks2, local2, terms2, remote_tiles)
    return (
        out.reshape(row_count, width),
        grad_weight,
        grad_features.reshape(row_count, width),
    )


def solution(mesh):
    rows = P(AXES, None)
    flat = P(AXES)
    tiles = P(AXES, None, None)
    in_specs = (rows, flat, flat, tiles, flat, flat, tiles, P(), rows)
    return jax.shard_map(
        body, mesh=mesh, in_specs=in_specs, out_specs=(rows, P(), rows), check_vma=False
    )
```

```python
import functools
import math

import jax
import jax.numpy as jnp
from jax import lax
from jax.experimental import pallas as pl
from jax.experimental.pallas import tpu as pltpu
from jax.sharding import PartitionSpec as P

BLOCK = 128
BLK_DEV = 16
AXES = ("group", "member")
VMEM = pl.BlockSpec(memory_space=pltpu.VMEM)
SMEM = pl.BlockSpec(memory_space=pltpu.SMEM)
MESH = pl.DeviceIdType.MESH
HBM = pl.BlockSpec(memory_space=pl.ANY)
LIMIT = 63 * 1024 * 1024


def dot(a, b):
    return jnp.dot(a, b, preferred_element_type=jnp.float32)


def dot_lt(a, b):
    return lax.dot_general(a, b, (((0,), (0,)), ((), ())), preferred_element_type=jnp.float32)


def dot_rt(a, b):
    return lax.dot_general(a, b, (((1,), (1,)), ((), ())), preferred_element_type=jnp.float32)


def fill_terms(v, pair, home_r, tiles_r, send, part=0, parts=1):
    count = send.shape[0] // 4 // parts

    @pl.loop(part * count, (part + 1) * count)
    def _(i):
        for j in range(4):
            k = i * 4 + j
            p = pair[k]
            send[k, send.shape[1] - BLOCK :] = dot_lt(tiles_r[p], v[home_r[p]]).astype(jnp.bfloat16)


def fill_blocks(v, asked, send):
    @pl.loop(0, send.shape[0] // 4)
    def _(i):
        for j in range(4):
            k = i * 4 + j
            send[k, :BLOCK] = v[jnp.maximum(asked[k], 0)]


def add_products(acc, came, home_r, target, tiles_r):
    @pl.loop(0, tiles_r.shape[0] // 4)
    def _(i):
        ps = [i * 4 + j for j in range(4)]
        terms = [dot(tiles_r[p], came[target[p], :BLOCK]) for p in ps]
        for p, term in zip(ps, terms):
            acc[home_r[p]] += term


def add_terms(acc, came, asked):
    first = came.shape[1] - BLOCK

    @pl.loop(0, came.shape[0])
    def _(j):
        @pl.when(asked[j] >= 0)
        def _():
            acc[asked[j]] += came[j, first:].astype(jnp.float32)


def begin(src, dst, sems, i):
    copy = pltpu.make_async_copy(src, dst, sems.at[i])
    copy.start()
    return copy


def place(index, members):
    return (index // members, lax.rem(index, members))


def send_kernel(members, home_r, pair, request, v, tiles_r, send, asked, came, seen, sent, got, local):
    devices = send.shape[0]
    me = lax.axis_index("group") * members + lax.axis_index("member")
    barrier = pltpu.get_barrier_semaphore()

    @pl.loop(1, devices)
    def _(k):
        pl.semaphore_signal(
            barrier, inc=1, device_id=place(lax.rem(me + k, devices), members), device_id_type=MESH
        )

    fill_terms(v, pair, home_r, tiles_r, send, 0, 2)
    pl.semaphore_wait(barrier, devices - 1)

    def copy(k, slot):
        peer = lax.rem(me + k, devices)
        row = me if slot is None else peer
        return pltpu.make_async_remote_copy(
            src_ref=request,
            dst_ref=came.at[row],
            send_sem=sent.at[peer],
            recv_sem=got.at[row],
            device_id=place(peer, members),
            device_id_type=MESH,
        )

    @pl.loop(1, devices)
    def _(k):
        copy(k, None).start()

    came[me] = request[...]
    fill_terms(v, pair, home_r, tiles_r, send, 1, 2)

    @pl.loop(1, devices)
    def _(k):
        copy(k, 1).wait()

    down = pltpu.make_async_copy(came, seen, local)
    down.start()
    down.wait()

    @pl.loop(0, devices)
    def _(j):
        asked[j] = seen[j, 0, me]

    @pl.loop(0, devices // 4)
    def _(i):
        for j in range(4):
            k = i * 4 + j
            send[k, :BLOCK] = v[jnp.maximum(seen[k, 0, me], 0)]


def local_sums(home, near, v, tiles, acc):
    @pl.loop(0, tiles.shape[0], unroll=2)
    def _(p):
        h, n = home[p], near[p]
        tile = tiles[p]
        acc[h] += dot(tile, v[n])
        acc[n] += dot_lt(tile, v[h])


def first_kernel(home, near, v, tiles, acc):
    acc[...] = jnp.zeros_like(acc)
    local_sums(home, near, v, tiles, acc)


STEP = 4


def gates(f, a, c, weight):
    width = f.shape[-1]
    z = dot(f, weight[:width]) + dot(a, weight[width:])
    s = jax.nn.sigmoid(z)
    g = (c.astype(jnp.float32) * s * (1.0 + z * (1.0 - s))).astype(jnp.bfloat16)
    return z * s, g


PARTS = 4


def middle_kernel(
    asked, home_r, target, pair, arrived_h, local_h, feats_h, cot_h, tiles_r, weight,
    agg_h, grad_agg_h, send_h, arrived, acc, feats, cot, agg, grad_agg, send, sems,
):
    copies = [
        begin(src, dst, sems, i)
        for i, (src, dst) in enumerate(
            [(arrived_h, arrived), (local_h, acc), (feats_h, feats), (cot_h, cot)]
        )
    ]
    width = feats.shape[-1]
    rows = STEP * BLOCK
    copies[0].wait()
    copies[1].wait()
    add_products(acc, arrived, home_r, target, tiles_r)
    add_terms(acc, arrived, asked)
    copies[2].wait()
    copies[3].wait()

    @pl.loop(0, feats.shape[0] // STEP)
    def _(i):
        sl = pl.ds(i * STEP, STEP)
        flat = lambda ref: ref[sl].reshape(rows, width)
        a = flat(acc).astype(jnp.bfloat16)
        agg[sl] = a.reshape(STEP, BLOCK, width)
        _, g = gates(flat(feats), a, flat(cot), weight)
        grad_agg[sl] = dot_rt(g, weight[width:]).astype(jnp.bfloat16).reshape(STEP, BLOCK, width)

    copies = [begin(agg, agg_h, sems, 4), begin(grad_agg, grad_agg_h, sems, 5)]
    size = send.shape[0] // PARTS
    for part in range(PARTS):
        fill_terms(grad_agg, pair, home_r, tiles_r, send, part, PARTS)
        sl = pl.ds(part * size, size)
        copies.append(begin(send.at[sl], send_h.at[sl], sems, 6 + part))
    for copy in copies:
        copy.wait()


def second_kernel(home, near, asked, feats, agg, cot, weight, grad_agg, tiles, out, acc, partial, send):
    width = feats.shape[-1]
    half = partial.shape[-1]
    rows = STEP * BLOCK
    fill_blocks(grad_agg, asked, send)
    partial[...] = jnp.zeros_like(partial)

    @pl.loop(0, feats.shape[0] // STEP)
    def _(i):
        sl = pl.ds(i * STEP, STEP)
        flat = lambda ref: ref[sl].reshape(rows, width)
        f, a = flat(feats), flat(agg)
        o, g = gates(f, a, flat(cot), weight)
        out[sl] = o.astype(jnp.bfloat16).reshape(STEP, BLOCK, width)
        for part in range(2):
            cols = g[:, part * half : (part + 1) * half]
            partial[part, :width] += dot_lt(f, cols)
            partial[part, width:] += dot_lt(a, cols)
        acc[sl] = dot_rt(g, weight[:width]).reshape(STEP, BLOCK, width)

    local_sums(home, near, grad_agg, tiles, acc)


def reduce_kernel(
    members, x, blocks, res, arrived, acc, came, send_sem, recv_sem, sent, got
):
    devices = blocks.shape[0]
    g, m = lax.axis_index("group"), lax.axis_index("member")
    me = g * members + m
    bits = members.bit_length() - 1
    peers, sides = [(1 - g, m)], []
    for b in range(bits):
        side = lax.rem(m // (1 << b), 2)
        sides.append(side)
        peers.append((g, m + (1 - 2 * side) * (1 << b)))
    barrier = pltpu.get_barrier_semaphore()

    @pl.loop(1, devices)
    def _(k):
        pl.semaphore_signal(
            barrier, inc=1, device_id=place(lax.rem(me + k, devices), members), device_id_type=MESH
        )

    pl.semaphore_wait(barrier, devices - 1)

    def block_copy(k, arriving):
        peer = lax.rem(me + k, devices)
        row = peer if arriving else me
        return pltpu.make_async_remote_copy(
            src_ref=blocks.at[peer],
            dst_ref=arrived.at[row],
            send_sem=sent.at[peer],
            recv_sem=got.at[row],
            device_id=place(peer, members),
            device_id_type=MESH,
        )

    trades = 2 * bits + 2

    def trade(src, dst, sem, peer):
        copy = pltpu.make_async_remote_copy(
            src_ref=src,
            dst_ref=dst,
            send_sem=send_sem.at[sem],
            recv_sem=recv_sem.at[sem],
            device_id=peer,
            device_id_type=MESH,
        )
        copy.start()
        first, end = (1 - (-i * (devices - 1)) // trades for i in (sem, sem + 1))

        @pl.loop(first, end)
        def _(k):
            block_copy(k, False).start()

        copy.wait()

    total = x.shape[1]
    trade(x.at[1 - g], came.at[pl.ds(0, total)], 0, peers[0])
    acc[...] = x[g] + came[:total]
    low, size, spot, lows = 0, total, total, []
    for b in range(bits):
        lows.append(low)
        size //= 2
        give = pl.multiple_of(low + (1 - sides[b]) * size, 8)
        keep = pl.multiple_of(low + sides[b] * size, 8)
        trade(acc.at[pl.ds(give, size)], came.at[pl.ds(spot, size)], 1 + b, peers[1 + b])
        acc[pl.ds(keep, size)] += came[spot : spot + size]
        low, spot = keep, spot + size
    res[g, pl.ds(low, size)] = acc[pl.ds(low, size)]
    for b in reversed(range(bits)):
        region = res.at[g, pl.ds(low, size)]
        trade(region, region, 2 * bits - b, peers[1 + b])
        low, size = lows[b], size * 2
    trade(res.at[g], res.at[g], 1 + 2 * bits, peers[0])

    @pl.loop(1, devices)
    def _(k):
        block_copy(k, True).wait()


def final_kernel(
    asked, home_r, target, blocks_h, local_h, terms_h, tiles_r, out_h, blocks, terms, acc, sems
):
    copies = [
        begin(src, dst, sems, i)
        for i, (src, dst) in enumerate([(blocks_h, blocks), (local_h, acc), (terms_h, terms)])
    ]
    copies[0].wait()
    copies[1].wait()
    add_products(acc, blocks, home_r, target, tiles_r)
    copies[2].wait()
    add_terms(acc, terms, asked)
    begin(acc, out_h, sems, 3).wait()


def call(kernel, out_shape, n_smem, n_vmem, scratch=(), flops=0, moved=0, out_specs=None, in_specs=None, cid=None):
    params = dict(vmem_limit_bytes=LIMIT)
    if cid is not None:
        params.update(collective_id=cid, has_side_effects=True)
    return pl.pallas_call(
        kernel,
        out_shape=out_shape,
        in_specs=in_specs or [SMEM] * n_smem + [VMEM] * n_vmem,
        out_specs=jax.tree.map(lambda _: VMEM, out_shape) if out_specs is None else out_specs,
        scratch_shapes=list(scratch),
        compiler_params=pltpu.CompilerParams(**params),
        cost_estimate=pl.CostEstimate(flops=flops, bytes_accessed=moved, transcendentals=0),
    )


def exchange(buffer):
    return lax.all_to_all(buffer, AXES, split_axis=0, concat_axis=0, tiled=True)


def body(
    features, local_home, local_near, local_tiles, remote_home, remote_far, remote_tiles, weight, cotangent
):
    devices = lax.axis_size(AXES)
    row_count, width = features.shape
    blocks = row_count // BLOCK
    bf16, f32 = jnp.bfloat16, jnp.float32
    shaped = lambda dtype: jax.ShapeDtypeStruct((blocks, BLOCK, width), dtype)
    send_shape = jax.ShapeDtypeStruct((devices, 2 * BLOCK, width), bf16)
    half_shape = jax.ShapeDtypeStruct((devices, BLOCK, width), bf16)
    target = remote_far // BLK_DEV
    pairs = remote_far.shape[0]
    members = devices // lax.axis_size("group")
    hit = target[None, :] == jnp.arange(devices, dtype=jnp.int32)[:, None]
    pair = jnp.sum(jnp.where(hit, jnp.arange(pairs, dtype=jnp.int32)[None, :], 0), axis=1)
    lanes = -(-devices // 128) * 128
    row_hit = target[None, :] == jnp.arange(lanes, dtype=jnp.int32)[:, None]
    request = jnp.sum(jnp.where(row_hit, (remote_far % BLK_DEV + 1)[None, :], 0), axis=1)[None, :] - 1
    feats = features.reshape(blocks, BLOCK, width)
    cot = cotangent.reshape(blocks, BLOCK, width)
    local_flops = 4 * BLOCK * BLOCK * width * local_tiles.shape[0]
    dma = pltpu.SemaphoreType.DMA

    send1, asked = call(
        functools.partial(send_kernel, members),
        (send_shape, jax.ShapeDtypeStruct((devices,), jnp.int32)),
        2,
        3,
        scratch=[
            pltpu.VMEM((devices, 1, lanes), jnp.int32),
            pltpu.SMEM((devices, 1, lanes), jnp.int32),
            dma((devices,)),
            dma((devices,)),
            dma(()),
        ],
        out_specs=(VMEM, SMEM),
        cid=0,
    )(remote_home, pair, request, feats, remote_tiles)
    idx = (asked, remote_home, target)
    arrived1 = exchange(send1)
    local1 = call(first_kernel, shaped(f32), 2, 2, flops=20 * local_flops, moved=20 << 20)(
        local_home, local_near, feats, local_tiles
    )
    field = lambda dtype: pltpu.VMEM((blocks, BLOCK, width), dtype)
    agg, grad_agg, send2 = call(
        middle_kernel,
        (shaped(bf16), shaped(bf16), half_shape),
        4,
        6,
        scratch=[pltpu.VMEM(send_shape.shape, bf16), field(f32)]
        + [field(bf16)] * 4
        + [pltpu.VMEM(half_shape.shape, bf16), dma((6 + PARTS,))],
        in_specs=[SMEM] * 4 + [HBM] * 4 + [VMEM] * 2,
        out_specs=(HBM,) * 3,
    )(*idx, pair, arrived1, local1, feats, cot, remote_tiles, weight)
    terms2 = exchange(send2)
    part = jax.ShapeDtypeStruct((2, weight.shape[0], width // 2), f32)
    out, local2, partial, send3 = call(
        second_kernel,
        (shaped(bf16), shaped(f32), part, half_shape),
        3,
        6,
        flops=20 * local_flops,
        moved=20 << 20,
    )(local_home, local_near, asked, feats, agg, cot, weight, grad_agg, local_tiles)
    steps = 2 * members.bit_length()
    summed, blocks2 = call(
        functools.partial(reduce_kernel, members),
        (part, half_shape),
        0,
        2,
        scratch=[
            pltpu.VMEM(part.shape[1:], f32),
            pltpu.VMEM((2 * part.shape[1], part.shape[2]), f32),
            dma((steps,)),
            dma((steps,)),
            dma((devices,)),
            dma((devices,)),
        ],
        flops=20 * local_flops,
        moved=20 << 20,
        in_specs=[VMEM, HBM],
        out_specs=(VMEM, HBM),
        cid=1,
    )(partial, send3)
    grad_scale = 1.0 / math.sqrt(row_count * devices)
    grad_weight = jnp.concatenate([summed[0], summed[1]], axis=1) * grad_scale
    grad_features = call(
        final_kernel,
        shaped(f32),
        3,
        4,
        scratch=[pltpu.VMEM(half_shape.shape, bf16)] * 2 + [field(f32), dma((4,))],
        in_specs=[SMEM] * 3 + [HBM] * 3 + [VMEM],
        out_specs=HBM,
    )(*idx, blocks2, local2, terms2, remote_tiles)
    return (
        out.reshape(row_count, width),
        grad_weight,
        grad_features.reshape(row_count, width),
    )


def solution(mesh):
    rows = P(AXES, None)
    flat = P(AXES)
    tiles = P(AXES, None, None)
    in_specs = (rows, flat, flat, tiles, flat, flat, tiles, P(), rows)
    return jax.shard_map(
        body, mesh=mesh, in_specs=in_specs, out_specs=(rows, P(), rows), check_vma=False
    )
```
